512 devices in a mesh: cell: 16 (over x_hi, z), sta: 32 (over x_lo, y, core).
Axes of the slice: x: 4 (x_hi: 2, x_lo: 2; x = x_hi * 2 + x_lo), y: 8, z: 8, core: 2. Of those that a mesh axis runs over, the one named last changes fastest.
Arguments:
- cell_index: int32 [3, 2048], P(None, 'cell'), may hold values from 0 to 127
- station_xyz: float32 [3, 256], P(None, 'sta'), may hold values from 0 to 2
- w_cell: float32 [3, 512], replicated, may hold values from -2.5 to 2.5
- w_station: float32 [3, 512], replicated, may hold values from -2.5 to 2.5
- bias_in: float32 [512], replicated, may hold values from -4 to 4
- w_hidden: bfloat16 [2, 512, 512], replicated, may hold values from -0.25 to 0.25
- bias_hidden: float32 [2, 512], replicated, may hold values from -3 to 3
- w_out: bfloat16 [512], replicated, may hold values from -0.25 to 0.25
- pick_mask: int32 [2048, 256], P('cell', 'sta'), may hold values 0 or 1
- arrival: float32 [2048, 256], P('cell', 'sta'), may hold values from 0 to 4
- quality: float32 [2048, 256], P('cell', 'sta'), may hold values from 0.002 to 2
Outputs:
- log_posterior: float32 [2048, 2048], P('sta', 'cell')
The draws below stay inside these ranges and needn't reach their ends.
All inputs are finite; a program needn't handle non-finite values. No bound on the sum of `pick_mask` on one device may be relied on, other than what follows from the above.
Results may differ from the reference program's by a relative error of at most 0.0011.
The reference program's roundings to bfloat16 on the way count: a program that leaves them out, or rounds other values in their place, can miss the bound.
Values sent between devices are 32-bit elements; how exact they have to be, the bound alone decides.
No kernel may reach another device: no remote copies, remote signals or barrier semaphores. Data moves between devices by JAX's collectives and lax.ppermute only.
A program may use at most 64 MiB of HBM per device.

```python
import math
import jax
import jax.numpy as jnp
from jax import lax

EVENTS = 2048
HID = 512
LAYERS = 2
CELLS = 2048
STATIONS = 256


def draw_quality(key, part):
    base = jnp.exp(jax.random.uniform(key, (EVENTS, STATIONS), jnp.float32, math.log(0.002), math.log(0.02)))
    return base


def place_ends(values, rng, least, high):
    longest = values.shape.index(max(values.shape))
    spots = []
    for shift in (0, 1):
        where = [jax.random.randint(jax.random.fold_in(rng, axis), (), 0, length) for axis, length in enumerate(values.shape)]
        where[longest] = (where[longest] + shift) % values.shape[longest]
        spots.append(tuple(where))
    return values.at[spots[0]].set(least).at[spots[1]].set(high)


def shard_levels(rng, dims, pieces, low, top_value):
    gain, own = 1.0, jax.random.fold_in(rng, 6)
    for axis_at, parts in pieces:
        steps = jnp.exp(jax.random.uniform(jax.random.fold_in(own, axis_at), (parts,), jnp.float32, low / len(pieces), top_value / len(pieces)))
        gain = gain * jnp.repeat(steps, dims[axis_at] // parts).reshape([-1 if axis == axis_at else 1 for axis in range(len(dims))])
    return gain


def bell_draw(key, extent, width, reach, dtype=jnp.bfloat16):
    array = jax.random.normal(key, extent, jnp.float32) * width
    return jnp.minimum(jnp.maximum(array, -reach), reach).astype(dtype)


def setup_inputs(seed: int = 0) -> dict:
    arg_keys = jax.random.split(jax.random.key(seed), 12)
    return {
        "cell_index": place_ends(jax.random.randint(arg_keys[0], (3, CELLS), 0, 128), jax.random.fold_in(arg_keys[0], 1), 0, 127).astype(jnp.int32),
        "station_xyz": jnp.clip(2.0 * jax.random.uniform(arg_keys[1], (3, STATIONS), jnp.float32) ** shard_levels(arg_keys[1], (3, STATIONS), ((1, 32),), -0.2, 0.2), 0.0, 2.0),
        "w_cell": bell_draw(arg_keys[2], (3, HID), 6 ** -0.5, 2.5, jnp.float32),
        "w_station": bell_draw(arg_keys[3], (3, HID), 6 ** -0.5, 2.5, jnp.float32),
        "bias_in": bell_draw(arg_keys[4], (HID,), 1.0, 4.0, jnp.float32),
        "w_hidden": bell_draw(arg_keys[5], (LAYERS, HID, HID), HID ** -0.5, 0.25),
        "bias_hidden": bell_draw(arg_keys[6], (LAYERS, HID), 0.5, 3.0, jnp.float32),
        "w_out": bell_draw(arg_keys[7], (HID,), HID ** -0.5, 0.25),
        "pick_mask": place_ends((jax.random.randint(arg_keys[8], (EVENTS, STATIONS), 0, 4) < 3).astype(jnp.int32), jax.random.fold_in(arg_keys[8], 1), 0, 1),
        "arrival": jnp.clip(4.0 * jax.random.uniform(arg_keys[9], (EVENTS, STATIONS), jnp.float32) ** shard_levels(arg_keys[9], (EVENTS, STATIONS), ((0, 16), (1, 32)), -0.2, 0.2), 0.0, 4.0),
        "quality": draw_quality(jax.random.fold_in(arg_keys[11], 71), 0),
    }


grid_step = 0.015625

def travel_times(cell_index, station_xyz, w_cell, w_station, bias_in, w_hidden, bias_hidden, w_out):
    highest = lax.Precision.HIGHEST
    cell_xyz = cell_index.astype(jnp.float32) * grid_step
    cell_count = cell_xyz.shape[1]
    station_count = station_xyz.shape[1]
    hidden_width = w_cell.shape[1]
    cell_rows = jnp.einsum('kc,kh->ch', cell_xyz, w_cell, precision=highest) + bias_in
    station_rows = jnp.einsum('ks,kh->sh', station_xyz, w_station, precision=highest)
    block_size = max(1, min(cell_count, 16384 // station_count))
    block_count = cell_count // block_size

    def one_block(block_item):
        rows_here, positions = block_item
        hidden = jax.nn.elu(rows_here[:, None, :] + station_rows[None, :, :]).astype(jnp.bfloat16)
        hidden = hidden.reshape(block_size * station_count, hidden_width)
        for layer_id in range(w_hidden.shape[0]):
            hidden = jax.nn.elu(jnp.dot(hidden, w_hidden[layer_id], preferred_element_type=jnp.float32) + bias_hidden[layer_id]).astype(jnp.bfloat16)
        output_raw = jnp.dot(hidden, w_out, preferred_element_type=jnp.float32).reshape(block_size, station_count)
        offsets = positions[:, :, None] - station_xyz[None, :, :]
        distance = jnp.sqrt(lax.optimization_barrier(jnp.sum(offsets * offsets, axis=1)))
        return distance * (0.25 + jax.nn.softplus(output_raw))
    blocks = (cell_rows.reshape(block_count, block_size, hidden_width), cell_xyz.T.reshape(block_count, block_size, 3))
    result = lax.map(one_block, blocks)
    return result.reshape(cell_count, station_count)

def reference(cell_index, station_xyz, w_cell, w_station, bias_in, w_hidden, bias_hidden, w_out, pick_mask, arrival, quality):
    highest = lax.Precision.HIGHEST
    travel = travel_times(cell_index, station_xyz, w_cell, w_station, bias_in, w_hidden, bias_hidden, w_out)
    weight = pick_mask.astype(jnp.float32) * quality
    weighted = weight * arrival
    curv = jnp.einsum('es,cs->ec', weight, travel * travel, precision=highest) - 2.0 * jnp.einsum('es,cs->ec', weighted, travel, precision=highest)
    lin = jnp.einsum('es,cs->ec', weight, travel, precision=highest)
    sq_sum = lax.optimization_barrier(jnp.sum(weighted * arrival, axis=1))
    mean_sum = lax.optimization_barrier(jnp.sum(weighted, axis=1))
    total_w = lax.optimization_barrier(jnp.sum(weight, axis=1))
    centered = mean_sum[:, None] - lin
    misfit = sq_sum[:, None] + curv - centered * centered / total_w[:, None]
    logit = -0.5 * misfit
    peak = lax.optimization_barrier(jnp.max(logit, axis=1))
    total = lax.optimization_barrier(jnp.sum(jnp.exp(logit - peak[:, None]), axis=1))
    return logit - peak[:, None] - jnp.log(total)[:, None]
```

```python
import jax
import jax.numpy as jnp
from jax import lax
from jax.experimental import pallas as pl
from jax.experimental.pallas import tpu as pltpu
from jax.sharding import PartitionSpec as P

grid_step = 0.015625
highest = lax.Precision.HIGHEST


def elu(x):
    return jnp.where(x > 0.0, x, jnp.exp(jnp.minimum(x, 0.0)) - 1.0)


def pack_kernel(mask_ref, arrival_ref, quality_ref, out_ref):
    weight = mask_ref[...].astype(jnp.float32) * quality_ref[...]
    arrival = arrival_ref[...]
    half = weight.shape[1] // 2
    for h in range(2):
        part = slice(h * half, (h + 1) * half)
        block = jnp.concatenate([weight[:, part], arrival[:, part]], axis=1)
        for peer in range(out_ref.shape[0]):
            out_ref[peer, h] = block


def travel_kernel(
    cell_ref,
    station_ref,
    w_cell_ref,
    w_station_ref,
    bias_in_ref,
    w_hidden_ref,
    bias_hidden_ref,
    w_out_ref,
    out_ref,
    hidden_ref,
):
    stations = station_ref.shape[1]
    cells = cell_ref.shape[1]
    cell = cell_ref[...].astype(jnp.float32) * grid_step
    cell_columns = cell.T
    station_columns = station_ref[...].T
    cell_rows = jnp.broadcast_to(bias_in_ref[...], (cells, bias_in_ref.shape[1]))
    station_rows = jnp.zeros((stations, bias_in_ref.shape[1]), jnp.float32)
    distance = jnp.zeros((stations, cells), jnp.float32)
    for k in range(3):
        cell_rows = cell_rows + cell_columns[:, k : k + 1] * w_cell_ref[k : k + 1, :]
        station_rows = station_rows + station_columns[:, k : k + 1] * w_station_ref[k : k + 1, :]
        offset = cell[k : k + 1, :] - station_columns[:, k : k + 1]
        distance = distance + offset * offset
    distance = jnp.sqrt(distance)
    for s in range(stations):
        hidden_ref[s * cells : (s + 1) * cells, :] = elu(cell_rows + station_rows[s : s + 1, :]).astype(
            jnp.bfloat16
        )
    hidden = hidden_ref[...]
    for layer in range(w_hidden_ref.shape[0]):
        hidden = elu(
            jnp.dot(hidden, w_hidden_ref[layer], preferred_element_type=jnp.float32)
            + bias_hidden_ref[layer : layer + 1, :]
        ).astype(jnp.bfloat16)
    raw = lax.dot_general(
        w_out_ref[...], hidden, (((1,), (1,)), ((), ())), preferred_element_type=jnp.float32
    )
    raw = jnp.concatenate([raw[:1, s * cells : (s + 1) * cells] for s in range(stations)], axis=0)
    softplus = jnp.maximum(raw, 0.0) + jnp.log1p(jnp.exp(-jnp.abs(raw)))
    out_ref[...] = distance * (0.25 + softplus)


def join_kernel(travel_ref, picks_ref, out_ref):
    travel = travel_ref[...]
    for peer in range(out_ref.shape[0]):
        out_ref[peer, 0] = travel
        out_ref[peer, 1] = picks_ref[peer]


def logit_kernel(blocks_ref, logit_ref, stats_ref):
    peers, _, rows, width = blocks_ref.shape
    half = width // 2
    travel = blocks_ref[:, 0].reshape(peers * rows, width)
    picks = blocks_ref[:, 1].reshape(peers * rows, width)
    weight, arrival = picks[:, :half], picks[:, half:]
    weighted = weight * arrival
    sq_sum = jnp.sum(weighted * arrival, axis=0, keepdims=True)
    mean_sum = jnp.sum(weighted, axis=0, keepdims=True)
    total_w = jnp.sum(weight, axis=0, keepdims=True)
    left = jnp.concatenate([travel * travel, travel], axis=1)
    right = jnp.concatenate([weight, weighted], axis=1)
    product = lax.dot_general(
        left, right, (((0,), (0,)), ((), ())), precision=highest, preferred_element_type=jnp.float32
    )
    curv = product[:width, :half] - 2.0 * product[width:, half:]
    lin = product[width:, :half]
    centered = mean_sum - lin
    logit = -0.5 * (sq_sum + curv - centered * centered / total_w)
    peak = jnp.max(logit, axis=0, keepdims=True)
    total = jnp.sum(jnp.exp(logit - peak), axis=0, keepdims=True)
    logit_ref[...] = logit
    stats = jnp.concatenate([peak, total], axis=1)
    for peer in range(stats_ref.shape[0]):
        stats_ref[peer] = stats


def final_kernel(logit_ref, stats_ref, out_ref):
    half = logit_ref.shape[1]
    peaks = stats_ref[:, 0, :half]
    totals = stats_ref[:, 0, half:]
    peak = jnp.max(peaks, axis=0, keepdims=True)
    total = jnp.sum(totals * jnp.exp(peaks - peak), axis=0, keepdims=True)
    out_ref[...] = (logit_ref[...] - peak - jnp.log(total)).T


def per_device(
    cell_index,
    station_xyz,
    w_cell,
    w_station,
    bias_in,
    w_hidden,
    bias_hidden,
    w_out,
    pick_mask,
    arrival,
    quality,
):
    n_cell, n_sta = lax.axis_size("cell"), lax.axis_size("sta")
    events, stations = pick_mask.shape
    cells = cell_index.shape[1]
    f32 = jnp.float32
    packed = pl.pallas_call(
        pack_kernel, out_shape=jax.ShapeDtypeStruct((n_cell, 2, stations, events), f32), name="pack"
    )(pick_mask.T, arrival.T, quality.T)
    picks = lax.all_to_all(packed, "cell", 0, 0)
    picks = picks.reshape(n_sta, stations, events)
    travel = pl.pallas_call(
        travel_kernel,
        out_shape=jax.ShapeDtypeStruct((stations, cells), f32),
        scratch_shapes=[pltpu.VMEM((stations * cells, w_cell.shape[1]), jnp.bfloat16)],
        compiler_params=pltpu.CompilerParams(vmem_limit_bytes=40 << 20),
        name="travel",
    )(
        cell_index,
        station_xyz,
        w_cell,
        w_station,
        bias_in[None],
        w_hidden,
        bias_hidden,
        w_out[None],
    )
    blocks = pl.pallas_call(
        join_kernel,
        out_shape=jax.ShapeDtypeStruct((n_sta, 2, stations, cells), f32),
        name="join",
    )(travel, picks)
    blocks = lax.all_to_all(blocks, "sta", 0, 0)
    logit, stats = pl.pallas_call(
        logit_kernel,
        out_shape=(
            jax.ShapeDtypeStruct((cells, events // 2), f32),
            jax.ShapeDtypeStruct((n_cell, 1, events), f32),
        ),
        compiler_params=pltpu.CompilerParams(vmem_limit_bytes=40 << 20),
        name="logit",
    )(blocks)
    stats = lax.all_to_all(stats, "cell", 0, 0)
    return pl.pallas_call(
        final_kernel, out_shape=jax.ShapeDtypeStruct((events // 2, cells), f32), name="final"
    )(logit, stats)


def solution(mesh):
    in_specs = (
        P(None, "cell"),
        P(None, "sta"),
        P(),
        P(),
        P(),
        P(),
        P(),
        P(),
        P("cell", "sta"),
        P("cell", "sta"),
        P("cell", "sta"),
    )
    return jax.shard_map(
        per_device, mesh=mesh, in_specs=in_specs, out_specs=P("sta", "cell"), check_vma=False
    )
```

```python
import jax
import jax.numpy as jnp
from jax import lax
from jax.experimental import pallas as pl
from jax.experimental.pallas import tpu as pltpu
from jax.sharding import PartitionSpec as P

grid_step = 0.015625
highest = lax.Precision.HIGHEST


def elu(x):
    return jnp.where(x > 0.0, x, jnp.exp(jnp.minimum(x, 0.0)) - 1.0)


def pack_kernel(mask_hbm, arrival_hbm, quality_hbm, out_ref, mask_ref, arrival_ref, quality_ref, sems):
    pairs = ((mask_hbm, mask_ref), (arrival_hbm, arrival_ref), (quality_hbm, quality_ref))
    copies = [pltpu.make_async_copy(*pair, sems.at[k]) for k, pair in enumerate(pairs)]
    for copy in copies:
        copy.start()
    for copy in copies:
        copy.wait()
    weight = mask_ref[...].astype(jnp.float32) * quality_ref[...]
    arrival = arrival_ref[...]
    half = weight.shape[1] // 2
    for h in range(2):
        part = slice(h * half, (h + 1) * half)
        block = jnp.concatenate([weight[:, part], arrival[:, part]], axis=1)
        for peer in range(out_ref.shape[0]):
            out_ref[peer, h] = block


def travel_kernel(
    cell_ref,
    station_ref,
    w_cell_ref,
    w_station_ref,
    bias_in_ref,
    w_hidden_hbm,
    bias_hidden_ref,
    w_out_ref,
    out_ref,
    w_hidden_ref,
    hidden_ref,
    sems,
):
    layers = w_hidden_ref.shape[0]
    copies = [
        pltpu.make_async_copy(w_hidden_hbm.at[layer], w_hidden_ref.at[layer], sems.at[layer])
        for layer in range(layers)
    ]
    for copy in copies:
        copy.start()
    stations = station_ref.shape[1]
    cells = cell_ref.shape[1]
    cell = cell_ref[...].astype(jnp.float32) * grid_step
    cell_columns = cell.T
    station_columns = station_ref[...].T
    cell_rows = jnp.broadcast_to(bias_in_ref[...], (cells, bias_in_ref.shape[1]))
    station_rows = jnp.zeros((stations, bias_in_ref.shape[1]), jnp.float32)
    distance = jnp.zeros((stations, cells), jnp.float32)
    for k in range(3):
        cell_rows = cell_rows + cell_columns[:, k : k + 1] * w_cell_ref[k : k + 1, :]
        station_rows = station_rows + station_columns[:, k : k + 1] * w_station_ref[k : k + 1, :]
        offset = cell[k : k + 1, :] - station_columns[:, k : k + 1]
        distance = distance + offset * offset
    distance = jnp.sqrt(distance)
    for s in range(stations):
        hidden_ref[s * cells : (s + 1) * cells, :] = elu(cell_rows + station_rows[s : s + 1, :]).astype(
            jnp.bfloat16
        )
    hidden = hidden_ref[...]
    for layer in range(layers):
        copies[layer].wait()
        hidden = elu(
            jnp.dot(hidden, w_hidden_ref[layer], preferred_element_type=jnp.float32)
            + bias_hidden_ref[layer : layer + 1, :]
        ).astype(jnp.bfloat16)
    raw = lax.dot_general(
        w_out_ref[...], hidden, (((1,), (1,)), ((), ())), preferred_element_type=jnp.float32
    )
    raw = jnp.concatenate([raw[:1, s * cells : (s + 1) * cells] for s in range(stations)], axis=0)
    softplus = jnp.maximum(raw, 0.0) + jnp.log1p(jnp.exp(-jnp.abs(raw)))
    out_ref[...] = distance * (0.25 + softplus)


def join_kernel(travel_ref, picks_ref, out_ref):
    travel = travel_ref[...]
    for peer in range(out_ref.shape[0]):
        out_ref[peer, 0] = travel
        out_ref[peer, 1] = picks_ref[peer]


def logit_kernel(blocks_ref, logit_ref, stats_ref):
    peers, _, rows, width = blocks_ref.shape
    half = width // 2
    travel = blocks_ref[:, 0].reshape(peers * rows, width)
    picks = blocks_ref[:, 1].reshape(peers * rows, width)
    weight, arrival = picks[:, :half], picks[:, half:]
    weighted = weight * arrival
    sq_sum = jnp.sum(weighted * arrival, axis=0, keepdims=True)
    mean_sum = jnp.sum(weighted, axis=0, keepdims=True)
    total_w = jnp.sum(weight, axis=0, keepdims=True)
    left = jnp.concatenate([travel * travel, travel], axis=1)
    right = jnp.concatenate([weight, weighted], axis=1)
    product = lax.dot_general(
        left, right, (((0,), (0,)), ((), ())), precision=highest, preferred_element_type=jnp.float32
    )
    curv = product[:width, :half] - 2.0 * product[width:, half:]
    lin = product[width:, :half]
    centered = mean_sum - lin
    logit = -0.5 * (sq_sum + curv - centered * centered / total_w)
    peak = jnp.max(logit, axis=0, keepdims=True)
    total = jnp.sum(jnp.exp(logit - peak), axis=0, keepdims=True)
    logit_ref[...] = logit
    stats = jnp.concatenate([peak, total], axis=1)
    for peer in range(stats_ref.shape[0]):
        stats_ref[peer] = stats


def final_kernel(logit_ref, stats_ref, out_ref):
    half = logit_ref.shape[1]
    peaks = stats_ref[:, 0, :half]
    totals = stats_ref[:, 0, half:]
    peak = jnp.max(peaks, axis=0, keepdims=True)
    total = jnp.sum(totals * jnp.exp(peaks - peak), axis=0, keepdims=True)
    out_ref[...] = (logit_ref[...] - peak - jnp.log(total)).T


vmem = pl.BlockSpec(memory_space=pltpu.VMEM)
hbm = pl.BlockSpec(memory_space=pltpu.HBM)


def in_hbm(x):
    return pltpu.with_memory_space_constraint(x, pltpu.HBM)


def call(kernel, in_specs, out_shape, name, scratch_shapes=()):
    return pl.pallas_call(
        kernel,
        in_specs=in_specs,
        out_specs=jax.tree.map(lambda _: vmem, out_shape),
        out_shape=out_shape,
        scratch_shapes=scratch_shapes,
        compiler_params=pltpu.CompilerParams(vmem_limit_bytes=40 << 20),
        name=name,
    )


def per_device(
    cell_index,
    station_xyz,
    w_cell,
    w_station,
    bias_in,
    w_hidden,
    bias_hidden,
    w_out,
    pick_mask,
    arrival,
    quality,
):
    n_cell, n_sta = lax.axis_size("cell"), lax.axis_size("sta")
    events, stations = pick_mask.shape
    cells = cell_index.shape[1]
    f32 = jnp.float32
    shape = jax.ShapeDtypeStruct
    packed = call(
        pack_kernel,
        [hbm] * 3,
        shape((n_cell, 2, stations, events), f32),
        "pack",
        [
            pltpu.VMEM((stations, events), pick_mask.dtype),
            pltpu.VMEM((stations, events), f32),
            pltpu.VMEM((stations, events), f32),
            pltpu.SemaphoreType.DMA((3,)),
        ],
    )(*[in_hbm(x.T) for x in (pick_mask, arrival, quality)])
    picks = lax.all_to_all(packed, "cell", 0, 0).reshape(n_sta, stations, events)
    travel = call(
        travel_kernel,
        [vmem] * 5 + [hbm] + [vmem] * 2,
        shape((stations, cells), f32),
        "travel",
        [
            pltpu.VMEM(w_hidden.shape, w_hidden.dtype),
            pltpu.VMEM((stations * cells, w_cell.shape[1]), jnp.bfloat16),
            pltpu.SemaphoreType.DMA((w_hidden.shape[0],)),
        ],
    )(
        cell_index,
        station_xyz,
        w_cell,
        w_station,
        bias_in[None],
        in_hbm(w_hidden),
        bias_hidden,
        w_out[None],
    )
    blocks = call(join_kernel, [vmem] * 2, shape((n_sta, 2, stations, cells), f32), "join")(travel, picks)
    blocks = lax.all_to_all(blocks, "sta", 0, 0)
    logit, stats = call(
        logit_kernel,
        [vmem],
        (shape((cells, events // 2), f32), shape((n_cell, 1, events), f32)),
        "logit",
    )(blocks)
    stats = lax.all_to_all(stats, "cell", 0, 0)
    return call(final_kernel, [vmem] * 2, shape((events // 2, cells), f32), "final")(logit, stats)


def solution(mesh):
    in_specs = (
        P(None, "cell"),
        P(None, "sta"),
        P(),
        P(),
        P(),
        P(),
        P(),
        P(),
        P("cell", "sta"),
        P("cell", "sta"),
        P("cell", "sta"),
    )
    return jax.shard_map(
        per_device, mesh=mesh, in_specs=in_specs, out_specs=P("sta", "cell"), check_vma=False
    )
```

```python
import jax
import jax.numpy as jnp
from jax import lax
from jax.experimental import pallas as pl
from jax.experimental.pallas import tpu as pltpu
from jax.sharding import PartitionSpec as P

grid_step = 0.015625
highest = lax.Precision.HIGHEST


def elu(x):
    return jnp.where(x > 0.0, x, jnp.exp(jnp.minimum(x, 0.0)) - 1.0)


def pack_kernel(mask_hbm, arrival_hbm, quality_hbm, out_ref, mask_ref, arrival_ref, quality_ref, sems):
    pairs = ((mask_hbm, mask_ref), (arrival_hbm, arrival_ref), (quality_hbm, quality_ref))
    copies = [pltpu.make_async_copy(*pair, sems.at[k]) for k, pair in enumerate(pairs)]
    for copy in copies:
        copy.start()
    for copy in copies:
        copy.wait()
    weight = mask_ref[...].astype(jnp.float32) * quality_ref[...]
    arrival = arrival_ref[...]
    half = weight.shape[1] // 2
    for h in range(2):
        part = slice(h * half, (h + 1) * half)
        block = jnp.concatenate([weight[:, part], arrival[:, part]], axis=1)
        for peer in range(out_ref.shape[0]):
            out_ref[peer, h] = block


def travel_kernel(
    cell_ref,
    station_ref,
    w_cell_ref,
    w_station_ref,
    bias_in_ref,
    w_hidden_hbm,
    bias_hidden_ref,
    w_out_ref,
    out_ref,
    w_hidden_ref,
    hidden_ref,
    sems,
):
    layers = w_hidden_ref.shape[0]
    copies = [
        pltpu.make_async_copy(w_hidden_hbm.at[layer], w_hidden_ref.at[layer], sems.at[layer])
        for layer in range(layers)
    ]
    for copy in copies:
        copy.start()
    stations = station_ref.shape[1]
    cells = cell_ref.shape[1]
    cell = cell_ref[...].astype(jnp.float32) * grid_step
    cell_columns = cell.T
    station_columns = station_ref[...].T
    cell_rows = jnp.broadcast_to(bias_in_ref[...], (cells, bias_in_ref.shape[1]))
    station_rows = jnp.zeros((stations, bias_in_ref.shape[1]), jnp.float32)
    distance = jnp.zeros((stations, cells), jnp.float32)
    for k in range(3):
        cell_rows = cell_rows + cell_columns[:, k : k + 1] * w_cell_ref[k : k + 1, :]
        station_rows = station_rows + station_columns[:, k : k + 1] * w_station_ref[k : k + 1, :]
        offset = cell[k : k + 1, :] - station_columns[:, k : k + 1]
        distance = distance + offset * offset
    distance = jnp.sqrt(distance)
    for s in range(stations):
        hidden_ref[s * cells : (s + 1) * cells, :] = elu(cell_rows + station_rows[s : s + 1, :]).astype(
            jnp.bfloat16
        )
    hidden = hidden_ref[...]
    for layer in range(layers):
        copies[layer].wait()
        hidden = elu(
            jnp.dot(hidden, w_hidden_ref[layer], preferred_element_type=jnp.float32)
            + bias_hidden_ref[layer : layer + 1, :]
        ).astype(jnp.bfloat16)
    raw = lax.dot_general(
        w_out_ref[...], hidden, (((1,), (1,)), ((), ())), preferred_element_type=jnp.float32
    )
    raw = jnp.concatenate([raw[:1, s * cells : (s + 1) * cells] for s in range(stations)], axis=0)
    softplus = jnp.maximum(raw, 0.0) + jnp.log1p(jnp.exp(-jnp.abs(raw)))
    out_ref[...] = distance * (0.25 + softplus)


def join_kernel(travel_ref, picks_ref, out_ref):
    travel = travel_ref[...]
    for peer in range(out_ref.shape[0]):
        out_ref[peer, 0] = travel
        for h in range(2):
            out_ref[peer, 1 + h] = picks_ref[peer, h]


def logit_kernel(blocks_ref, logit_ref, stats_ref):
    cores, peers, _, rows, width = blocks_ref.shape
    half = width // 2
    odd = lax.axis_index("sta") % 2 == 1
    travel = blocks_ref[:, :, 0].reshape(cores * peers * rows, width)
    picks = jnp.where(odd, blocks_ref[:, :, 2], blocks_ref[:, :, 1]).reshape(cores * peers * rows, width)
    weight, arrival = picks[:, :half], picks[:, half:]
    weighted = weight * arrival
    sq_sum = jnp.sum(weighted * arrival, axis=0, keepdims=True)
    mean_sum = jnp.sum(weighted, axis=0, keepdims=True)
    total_w = jnp.sum(weight, axis=0, keepdims=True)
    left = jnp.concatenate([travel * travel, travel], axis=1)
    right = jnp.concatenate([weight, weighted], axis=1)
    product = lax.dot_general(
        left, right, (((0,), (0,)), ((), ())), precision=highest, preferred_element_type=jnp.float32
    )
    curv = product[:width, :half] - 2.0 * product[width:, half:]
    lin = product[width:, :half]
    centered = mean_sum - lin
    logit = -0.5 * (sq_sum + curv - centered * centered / total_w)
    peak = jnp.max(logit, axis=0, keepdims=True)
    total = jnp.sum(jnp.exp(logit - peak), axis=0, keepdims=True)
    logit_ref[...] = logit
    stats = jnp.concatenate([peak, total], axis=1)
    for peer in range(stats_ref.shape[0]):
        stats_ref[peer] = stats


def final_kernel(logit_ref, stats_ref, out_ref):
    half = logit_ref.shape[1]
    peaks = stats_ref[:, 0, :half]
    totals = stats_ref[:, 0, half:]
    peak = jnp.max(peaks, axis=0, keepdims=True)
    total = jnp.sum(totals * jnp.exp(peaks - peak), axis=0, keepdims=True)
    out_ref[...] = (logit_ref[...] - peak - jnp.log(total)).T


vmem = pl.BlockSpec(memory_space=pltpu.VMEM)
hbm = pl.BlockSpec(memory_space=pltpu.HBM)


def in_hbm(x):
    return pltpu.with_memory_space_constraint(x, pltpu.HBM)


def call(kernel, in_specs, out_shape, name, scratch_shapes=()):
    return pl.pallas_call(
        kernel,
        in_specs=in_specs,
        out_specs=jax.tree.map(lambda _: vmem, out_shape),
        out_shape=out_shape,
        scratch_shapes=scratch_shapes,
        compiler_params=pltpu.CompilerParams(vmem_limit_bytes=40 << 20),
        name=name,
    )


def per_device(
    cell_index,
    station_xyz,
    w_cell,
    w_station,
    bias_in,
    w_hidden,
    bias_hidden,
    w_out,
    pick_mask,
    arrival,
    quality,
):
    n_cell, n_sta = lax.axis_size("cell"), lax.axis_size("sta")
    events, stations = pick_mask.shape
    cells = cell_index.shape[1]
    f32 = jnp.float32
    shape = jax.ShapeDtypeStruct
    packed = call(
        pack_kernel,
        [hbm] * 3,
        shape((n_cell, 2, stations, events), f32),
        "pack",
        [
            pltpu.VMEM((stations, events), pick_mask.dtype),
            pltpu.VMEM((stations, events), f32),
            pltpu.VMEM((stations, events), f32),
            pltpu.SemaphoreType.DMA((3,)),
        ],
    )(*[in_hbm(x.T) for x in (pick_mask, arrival, quality)])
    picks = lax.all_to_all(packed, "cell", 0, 0)
    travel = call(
        travel_kernel,
        [vmem] * 5 + [hbm] + [vmem] * 2,
        shape((stations, cells), f32),
        "travel",
        [
            pltpu.VMEM(w_hidden.shape, w_hidden.dtype),
            pltpu.VMEM((stations * cells, w_cell.shape[1]), jnp.bfloat16),
            pltpu.SemaphoreType.DMA((w_hidden.shape[0],)),
        ],
    )(
        cell_index,
        station_xyz,
        w_cell,
        w_station,
        bias_in[None],
        in_hbm(w_hidden),
        bias_hidden,
        w_out[None],
    )
    blocks = call(join_kernel, [vmem] * 2, shape((n_cell, 3, stations, cells), f32), "join")(travel, picks)
    equal_cores = [list(range(core, n_sta, 2)) for core in range(2)]
    pairs = [[chip, chip + 1] for chip in range(0, n_sta, 2)]
    blocks = lax.all_to_all(blocks, "sta", 0, 0, axis_index_groups=equal_cores)
    blocks = lax.all_gather(blocks, "sta", axis_index_groups=pairs)
    logit, stats = call(
        logit_kernel,
        [vmem],
        (shape((cells, events // 2), f32), shape((n_cell, 1, events), f32)),
        "logit",
    )(blocks)
    stats = lax.all_to_all(stats, "cell", 0, 0)
    return call(final_kernel, [vmem] * 2, shape((events // 2, cells), f32), "final")(logit, stats)


def solution(mesh):
    in_specs = (
        P(None, "cell"),
        P(None, "sta"),
        P(),
        P(),
        P(),
        P(),
        P(),
        P(),
        P("cell", "sta"),
        P("cell", "sta"),
        P("cell", "sta"),
    )
    return jax.shard_map(
        per_device, mesh=mesh, in_specs=in_specs, out_specs=P("sta", "cell"), check_vma=False
    )
```

```python
import jax
import jax.numpy as jnp
from jax import lax
from jax.experimental import pallas as pl
from jax.experimental.pallas import tpu as pltpu
from jax.sharding import PartitionSpec as P

grid_step = 0.015625
highest = lax.Precision.HIGHEST


def elu(x):
    return jnp.where(x > 0.0, x, jnp.exp(jnp.minimum(x, 0.0)) - 1.0)


def pack_kernel(mask_hbm, arrival_hbm, quality_hbm, out_ref, mask_ref, arrival_ref, quality_ref, sems):
    pairs = ((mask_hbm, mask_ref), (arrival_hbm, arrival_ref), (quality_hbm, quality_ref))
    copies = [pltpu.make_async_copy(*pair, sems.at[k]) for k, pair in enumerate(pairs)]
    for copy in copies:
        copy.start()
    for copy in copies:
        copy.wait()
    weight = mask_ref[...].astype(jnp.float32) * quality_ref[...]
    arrival = arrival_ref[...]
    for peer in range(out_ref.shape[0]):
        out_ref[peer, 0] = weight
        out_ref[peer, 1] = arrival


def travel_kernel(
    cell_ref,
    station_ref,
    w_cell_ref,
    w_station_ref,
    bias_in_ref,
    w_hidden_ref,
    bias_hidden_hbm,
    w_out_ref,
    out_ref,
    hidden_ref,
    bias_hidden_ref,
    sem,
):
    bias_copy = pltpu.make_async_copy(bias_hidden_hbm, bias_hidden_ref, sem)
    bias_copy.start()
    stations = station_ref.shape[1]
    cells = cell_ref.shape[1]
    cell = cell_ref[...].astype(jnp.float32) * grid_step
    cell_columns = cell.T
    station_columns = station_ref[...].T
    cell_rows = jnp.broadcast_to(bias_in_ref[...], (cells, bias_in_ref.shape[1]))
    station_rows = jnp.zeros((stations, bias_in_ref.shape[1]), jnp.float32)
    distance = jnp.zeros((stations, cells), jnp.float32)
    for k in range(3):
        cell_rows = cell_rows + cell_columns[:, k : k + 1] * w_cell_ref[k : k + 1, :]
        station_rows = station_rows + station_columns[:, k : k + 1] * w_station_ref[k : k + 1, :]
        offset = cell[k : k + 1, :] - station_columns[:, k : k + 1]
        distance = distance + offset * offset
    distance = jnp.sqrt(distance)
    for s in range(stations):
        hidden_ref[s * cells : (s + 1) * cells, :] = elu(cell_rows + station_rows[s : s + 1, :]).astype(
            jnp.bfloat16
        )
    hidden = hidden_ref[...]
    bias_copy.wait()
    for layer in range(w_hidden_ref.shape[0]):
        hidden = elu(
            jnp.dot(hidden, w_hidden_ref[layer], preferred_element_type=jnp.float32)
            + bias_hidden_ref[layer : layer + 1, :]
        ).astype(jnp.bfloat16)
    raw = lax.dot_general(
        w_out_ref[...], hidden, (((1,), (1,)), ((), ())), preferred_element_type=jnp.float32
    )
    raw = jnp.concatenate([raw[:1, s * cells : (s + 1) * cells] for s in range(stations)], axis=0)
    softplus = jnp.maximum(raw, 0.0) + jnp.log1p(jnp.exp(-jnp.abs(raw)))
    out_ref[...] = distance * (0.25 + softplus)


def join_kernel(travel_ref, picks_ref, out_ref):
    travel = travel_ref[...]
    for peer in range(out_ref.shape[0]):
        out_ref[peer, 0] = travel
        for k in range(2):
            out_ref[peer, 1 + k] = picks_ref[peer, k]


def logit_kernel(blocks_ref, logit_ref, stats_ref):
    cores, peers, _, rows, width = blocks_ref.shape
    half = width // 2
    odd = lax.axis_index("sta") % 2 == 1
    travel = blocks_ref[:, :, 0].reshape(cores * peers * rows, width)
    weight, arrival = [
        jnp.where(odd, member[:, half:], member[:, :half])
        for member in [blocks_ref[:, :, k].reshape(cores * peers * rows, width) for k in (1, 2)]
    ]
    weighted = weight * arrival
    sq_sum = jnp.sum(weighted * arrival, axis=0, keepdims=True)
    mean_sum = jnp.sum(weighted, axis=0, keepdims=True)
    total_w = jnp.sum(weight, axis=0, keepdims=True)
    left = jnp.concatenate([travel * travel, travel], axis=1)
    right = jnp.concatenate([weight, weighted], axis=1)
    product = lax.dot_general(
        left, right, (((0,), (0,)), ((), ())), precision=highest, preferred_element_type=jnp.float32
    )
    curv = product[:width, :half] - 2.0 * product[width:, half:]
    lin = product[width:, :half]
    centered = mean_sum - lin
    logit = -0.5 * (sq_sum + curv - centered * centered / total_w)
    peak = jnp.max(logit, axis=0, keepdims=True)
    total = jnp.sum(jnp.exp(logit - peak), axis=0, keepdims=True)
    logit_ref[...] = logit
    stats = jnp.concatenate([peak, total], axis=1)
    for peer in range(stats_ref.shape[0]):
        stats_ref[peer] = stats


def final_kernel(logit_ref, stats_ref, out_ref):
    half = logit_ref.shape[1]
    peaks = stats_ref[:, 0, :half]
    totals = stats_ref[:, 0, half:]
    peak = jnp.max(peaks, axis=0, keepdims=True)
    total = jnp.sum(totals * jnp.exp(peaks - peak), axis=0, keepdims=True)
    out_ref[...] = (logit_ref[...] - peak - jnp.log(total)).T


vmem = pl.BlockSpec(memory_space=pltpu.VMEM)
hbm = pl.BlockSpec(memory_space=pltpu.HBM)


def in_hbm(x):
    return pltpu.with_memory_space_constraint(x, pltpu.HBM)


def call(kernel, in_specs, out_shape, name, scratch_shapes=(), cost=None):
    return pl.pallas_call(
        kernel,
        in_specs=in_specs,
        out_specs=jax.tree.map(lambda _: vmem, out_shape),
        out_shape=out_shape,
        scratch_shapes=scratch_shapes,
        compiler_params=pltpu.CompilerParams(vmem_limit_bytes=40 << 20),
        name=name,
        cost_estimate=cost,
    )


def per_device(
    cell_index,
    station_xyz,
    w_cell,
    w_station,
    bias_in,
    w_hidden,
    bias_hidden,
    w_out,
    pick_mask,
    arrival,
    quality,
):
    n_cell, n_sta = lax.axis_size("cell"), lax.axis_size("sta")
    events, stations = pick_mask.shape
    cells = cell_index.shape[1]
    f32 = jnp.float32
    shape = jax.ShapeDtypeStruct
    packed = call(
        pack_kernel,
        [hbm] * 3,
        shape((n_cell, 2, stations, events), f32),
        "pack",
        [
            pltpu.VMEM((stations, events), pick_mask.dtype),
            pltpu.VMEM((stations, events), f32),
            pltpu.VMEM((stations, events), f32),
            pltpu.SemaphoreType.DMA((3,)),
        ],
        pl.CostEstimate(flops=2 * 10**9, transcendentals=0, bytes_accessed=10**6),
    )(*[in_hbm(x.T) for x in (pick_mask, arrival, quality)])
    picks = lax.all_to_all(packed, "cell", 0, 0)
    travel = call(
        travel_kernel,
        [vmem] * 6 + [hbm, vmem],
        shape((stations, cells), f32),
        "travel",
        [
            pltpu.VMEM((stations * cells, w_cell.shape[1]), jnp.bfloat16),
            pltpu.VMEM(bias_hidden.shape, f32),
            pltpu.SemaphoreType.DMA,
        ],
    )(
        cell_index,
        station_xyz,
        w_cell,
        w_station,
        bias_in[None],
        w_hidden,
        in_hbm(bias_hidden),
        w_out[None],
    )
    blocks = call(join_kernel, [vmem] * 2, shape((n_cell, 3, stations, cells), f32), "join")(travel, picks)
    equal_cores = [list(range(core, n_sta, 2)) for core in range(2)]
    pairs = [[chip, chip + 1] for chip in range(0, n_sta, 2)]
    blocks = lax.all_to_all(blocks, "sta", 0, 0, axis_index_groups=equal_cores)
    blocks = lax.all_gather(blocks, "sta", axis_index_groups=pairs)
    logit, stats = call(
        logit_kernel,
        [vmem],
        (shape((cells, events // 2), f32), shape((n_cell, 1, events), f32)),
        "logit",
    )(blocks)
    stats = lax.all_to_all(stats, "cell", 0, 0)
    return call(final_kernel, [vmem] * 2, shape((events // 2, cells), f32), "final")(logit, stats)


def solution(mesh):
    in_specs = (
        P(None, "cell"),
        P(None, "sta"),
        P(),
        P(),
        P(),
        P(),
        P(),
        P(),
        P("cell", "sta"),
        P("cell", "sta"),
        P("cell", "sta"),
    )
    return jax.shard_map(
        per_device, mesh=mesh, in_specs=in_specs, out_specs=P("sta", "cell"), check_vma=False
    )
```

```python
import jax
import jax.numpy as jnp
from jax import lax
from jax.experimental import pallas as pl
from jax.experimental.pallas import tpu as pltpu
from jax.sharding import PartitionSpec as P

grid_step = 0.015625
highest = lax.Precision.HIGHEST


def elu(x):
    return jnp.where(x > 0.0, x, jnp.exp(jnp.minimum(x, 0.0)) - 1.0)


def pack_kernel(mask_hbm, arrival_hbm, quality_hbm, out_ref, mask_ref, arrival_ref, quality_ref, sems):
    pairs = ((mask_hbm, mask_ref), (arrival_hbm, arrival_ref), (quality_hbm, quality_ref))
    copies = [pltpu.make_async_copy(*pair, sems.at[k]) for k, pair in enumerate(pairs)]
    for copy in copies:
        copy.start()
    for copy in copies:
        copy.wait()
    weight = mask_ref[...].astype(jnp.float32) * quality_ref[...]
    arrival = arrival_ref[...]
    for peer in range(out_ref.shape[0]):
        out_ref[peer, 0] = weight
        out_ref[peer, 1] = arrival


def travel_kernel(
    cell_ref,
    station_ref,
    w_cell_ref,
    w_station_ref,
    bias_in_ref,
    w_hidden_ref,
    bias_hidden_hbm,
    w_out_ref,
    out_ref,
    hidden_ref,
    bias_hidden_ref,
    sem,
):
    bias_copy = pltpu.make_async_copy(bias_hidden_hbm, bias_hidden_ref, sem)
    bias_copy.start()
    stations = station_ref.shape[1]
    cells = cell_ref.shape[1]
    cell = cell_ref[...].astype(jnp.float32) * grid_step
    cell_columns = cell.T
    station_columns = station_ref[...].T
    cell_rows = jnp.broadcast_to(bias_in_ref[...], (cells, bias_in_ref.shape[1]))
    station_rows = jnp.zeros((stations, bias_in_ref.shape[1]), jnp.float32)
    distance = jnp.zeros((stations, cells), jnp.float32)
    for k in range(3):
        cell_rows = cell_rows + cell_columns[:, k : k + 1] * w_cell_ref[k : k + 1, :]
        station_rows = station_rows + station_columns[:, k : k + 1] * w_station_ref[k : k + 1, :]
        offset = cell[k : k + 1, :] - station_columns[:, k : k + 1]
        distance = distance + offset * offset
    distance = jnp.sqrt(distance)
    for s in range(stations):
        hidden_ref[s * cells : (s + 1) * cells, :] = elu(cell_rows + station_rows[s : s + 1, :]).astype(
            jnp.bfloat16
        )
    hidden = hidden_ref[...]
    bias_copy.wait()
    for layer in range(w_hidden_ref.shape[0]):
        hidden = elu(
            jnp.dot(hidden, w_hidden_ref[layer], preferred_element_type=jnp.float32)
            + bias_hidden_ref[layer : layer + 1, :]
        ).astype(jnp.bfloat16)
    raw = lax.dot_general(
        w_out_ref[...], hidden, (((1,), (1,)), ((), ())), preferred_element_type=jnp.float32
    )
    raw = jnp.concatenate([raw[:1, s * cells : (s + 1) * cells] for s in range(stations)], axis=0)
    softplus = jnp.maximum(raw, 0.0) + jnp.log1p(jnp.exp(-jnp.abs(raw)))
    out_ref[...] = distance * (0.25 + softplus)


def join_kernel(travel_ref, picks_ref, out_ref):
    travel = travel_ref[...]
    for peer in range(out_ref.shape[0]):
        out_ref[peer, 0] = travel
        for k in range(2):
            out_ref[peer, 1 + k] = picks_ref[peer, k]


def logit_kernel(blocks_ref, logit_ref, stats_ref):
    cores, peers, _, rows, width = blocks_ref.shape
    half = width // 2
    odd = lax.axis_index("sta") % 2 == 1
    travel, weight, arrival = [
        blocks_ref[:, :, k].reshape(cores * peers * rows, width) for k in range(3)
    ]
    weight, arrival = [
        jnp.where(odd, member[half:], member[:half]) for member in (weight.T, arrival.T)
    ]
    weighted = weight * arrival
    sq_sum = jnp.sum(weighted * arrival, axis=1, keepdims=True)
    mean_sum = jnp.sum(weighted, axis=1, keepdims=True)
    total_w = jnp.sum(weight, axis=1, keepdims=True)
    product = jnp.dot(
        jnp.concatenate([weight, weighted], axis=0),
        jnp.concatenate([travel * travel, travel], axis=1),
        precision=highest,
        preferred_element_type=jnp.float32,
    )
    curv = product[:half, :width] - 2.0 * product[half:, width:]
    centered = mean_sum - product[:half, width:]
    logit = -0.5 * (sq_sum + curv - centered * centered / total_w)
    peak = jnp.max(logit, axis=1, keepdims=True)
    total = jnp.sum(jnp.exp(logit - peak), axis=1, keepdims=True)
    logit_ref[...] = logit
    lane = lax.broadcasted_iota(jnp.int32, logit.shape, 1)
    rows = jnp.where(lane == 0, peak, total).T
    stats = jnp.concatenate([rows[:1], rows[1:2]], axis=1)
    for peer in range(stats_ref.shape[0]):
        stats_ref[peer] = stats


def final_kernel(logit_ref, stats_ref, out_ref):
    half = logit_ref.shape[0]
    peaks = stats_ref[:, 0, :half]
    totals = stats_ref[:, 0, half:]
    peak = jnp.max(peaks, axis=0, keepdims=True)
    total = jnp.sum(totals * jnp.exp(peaks - peak), axis=0, keepdims=True)
    row = lax.broadcasted_iota(jnp.int32, (8, peaks.shape[1]), 0)
    columns = jnp.where(row == 0, peak, jnp.log(total)).T
    out_ref[...] = logit_ref[...] - columns[:, :1] - columns[:, 1:2]


vmem = pl.BlockSpec(memory_space=pltpu.VMEM)
hbm = pl.BlockSpec(memory_space=pltpu.HBM)


def in_hbm(x):
    return pltpu.with_memory_space_constraint(x, pltpu.HBM)


def call(kernel, in_specs, out_shape, name, scratch_shapes=(), cost=None):
    return pl.pallas_call(
        kernel,
        in_specs=in_specs,
        out_specs=jax.tree.map(lambda _: vmem, out_shape),
        out_shape=out_shape,
        scratch_shapes=scratch_shapes,
        compiler_params=pltpu.CompilerParams(vmem_limit_bytes=40 << 20),
        name=name,
        cost_estimate=cost,
    )


def per_device(
    cell_index,
    station_xyz,
    w_cell,
    w_station,
    bias_in,
    w_hidden,
    bias_hidden,
    w_out,
    pick_mask,
    arrival,
    quality,
):
    n_cell, n_sta = lax.axis_size("cell"), lax.axis_size("sta")
    events, stations = pick_mask.shape
    cells = cell_index.shape[1]
    f32 = jnp.float32
    shape = jax.ShapeDtypeStruct
    packed = call(
        pack_kernel,
        [hbm] * 3,
        shape((n_cell, 2, stations, events), f32),
        "pack",
        [
            pltpu.VMEM((stations, events), pick_mask.dtype),
            pltpu.VMEM((stations, events), f32),
            pltpu.VMEM((stations, events), f32),
            pltpu.SemaphoreType.DMA((3,)),
        ],
        pl.CostEstimate(flops=2 * 10**9, transcendentals=0, bytes_accessed=10**6),
    )(*[in_hbm(x.T) for x in (pick_mask, arrival, quality)])
    picks = lax.all_to_all(packed, "cell", 0, 0)
    travel = call(
        travel_kernel,
        [vmem] * 6 + [hbm, vmem],
        shape((stations, cells), f32),
        "travel",
        [
            pltpu.VMEM((stations * cells, w_cell.shape[1]), jnp.bfloat16),
            pltpu.VMEM(bias_hidden.shape, f32),
            pltpu.SemaphoreType.DMA,
        ],
    )(
        cell_index,
        station_xyz,
        w_cell,
        w_station,
        bias_in[None],
        w_hidden,
        in_hbm(bias_hidden),
        w_out[None],
    )
    blocks = call(join_kernel, [vmem] * 2, shape((n_cell, 3, stations, cells), f32), "join")(travel, picks)
    equal_cores = [list(range(core, n_sta, 2)) for core in range(2)]
    pairs = [[chip, chip + 1] for chip in range(0, n_sta, 2)]
    blocks = lax.all_to_all(blocks, "sta", 0, 0, axis_index_groups=equal_cores)
    blocks = lax.all_gather(blocks, "sta", axis_index_groups=pairs)
    logit, stats = call(
        logit_kernel,
        [vmem],
        (shape((events // 2, cells), f32), shape((n_cell, 1, events), f32)),
        "logit",
    )(blocks)
    stats = lax.all_to_all(stats, "cell", 0, 0)
    return call(final_kernel, [vmem] * 2, shape((events // 2, cells), f32), "final")(logit, stats)


def solution(mesh):
    in_specs = (
        P(None, "cell"),
        P(None, "sta"),
        P(),
        P(),
        P(),
        P(),
        P(),
        P(),
        P("cell", "sta"),
        P("cell", "sta"),
        P("cell", "sta"),
    )
    return jax.shard_map(
        per_device, mesh=mesh, in_specs=in_specs, out_specs=P("sta", "cell"), check_vma=False
    )
```

```python
import jax
import jax.numpy as jnp
from jax import lax
from jax.experimental import pallas as pl
from jax.experimental.pallas import tpu as pltpu
from jax.sharding import PartitionSpec as P

grid_step = 0.015625
first_picks, first_blocks, first_stats = 12, 12, 12
pair_order = (0, 1)
highest = lax.Precision.HIGHEST


def elu(x):
    return jnp.where(x > 0.0, x, jnp.exp(jnp.minimum(x, 0.0)) - 1.0)


def pack_kernel(mask_hbm, arrival_hbm, quality_hbm, out_ref, mask_ref, arrival_ref, quality_ref, sems):
    pairs = ((mask_hbm, mask_ref), (arrival_hbm, arrival_ref), (quality_hbm, quality_ref))
    copies = [pltpu.make_async_copy(*pair, sems.at[k]) for k, pair in enumerate(pairs)]
    for copy in copies:
        copy.start()
    for copy in copies:
        copy.wait()
    weight = mask_ref[...].astype(jnp.float32) * quality_ref[...]
    arrival = arrival_ref[...]
    for peer in range(out_ref.shape[0]):
        out_ref[peer, 0] = weight
        out_ref[peer, 1] = arrival


def travel_kernel(
    cell_ref,
    station_ref,
    w_cell_ref,
    w_station_ref,
    bias_in_ref,
    w_hidden_ref,
    bias_hidden_hbm,
    w_out_ref,
    out_ref,
    hidden_ref,
    bias_hidden_ref,
    sem,
):
    bias_copy = pltpu.make_async_copy(bias_hidden_hbm, bias_hidden_ref, sem)
    bias_copy.start()
    stations = station_ref.shape[1]
    cells = cell_ref.shape[1]
    cell = cell_ref[...].astype(jnp.float32) * grid_step
    cell_columns = cell.T
    station_columns = station_ref[...].T
    cell_rows = jnp.broadcast_to(bias_in_ref[...], (cells, bias_in_ref.shape[1]))
    station_rows = jnp.zeros((stations, bias_in_ref.shape[1]), jnp.float32)
    distance = jnp.zeros((stations, cells), jnp.float32)
    for k in range(3):
        cell_rows = cell_rows + cell_columns[:, k : k + 1] * w_cell_ref[k : k + 1, :]
        station_rows = station_rows + station_columns[:, k : k + 1] * w_station_ref[k : k + 1, :]
        offset = cell[k : k + 1, :] - station_columns[:, k : k + 1]
        distance = distance + offset * offset
    distance = jnp.sqrt(distance)
    for s in range(stations):
        hidden_ref[s * cells : (s + 1) * cells, :] = elu(cell_rows + station_rows[s : s + 1, :]).astype(
            jnp.bfloat16
        )
    hidden = hidden_ref[...]
    bias_copy.wait()
    for layer in range(w_hidden_ref.shape[0]):
        hidden = elu(
            jnp.dot(hidden, w_hidden_ref[layer], preferred_element_type=jnp.float32)
            + bias_hidden_ref[layer : layer + 1, :]
        ).astype(jnp.bfloat16)
    raw = lax.dot_general(
        w_out_ref[...], hidden, (((1,), (1,)), ((), ())), preferred_element_type=jnp.float32
    )
    raw = jnp.concatenate([raw[:1, s * cells : (s + 1) * cells] for s in range(stations)], axis=0)
    softplus = jnp.maximum(raw, 0.0) + jnp.log1p(jnp.exp(-jnp.abs(raw)))
    out_ref[...] = distance * (0.25 + softplus)


def rotated(count, first):
    return [(first + place) % count for place in range(count)]


def join_kernel(travel_ref, picks_ref, out_ref):
    travel = travel_ref[...]
    peers = out_ref.shape[0]
    for place, chip in enumerate(rotated(peers, first_blocks)):
        out_ref[place, 0] = travel
        for k in range(2):
            out_ref[place, 1 + k] = picks_ref[rotated(peers, first_picks).index(chip), k]


def logit_kernel(blocks_ref, logit_ref, stats_ref):
    cores, peers, _, rows, width = blocks_ref.shape
    half = width // 2
    odd = lax.axis_index("sta") % 2 == 1
    travel, weight, arrival = [
        blocks_ref[:, :, k].reshape(cores * peers * rows, width) for k in range(3)
    ]
    weight, arrival = [
        jnp.where(odd, member[half:], member[:half]) for member in (weight.T, arrival.T)
    ]
    weighted = weight * arrival
    sq_sum = jnp.sum(weighted * arrival, axis=1, keepdims=True)
    mean_sum = jnp.sum(weighted, axis=1, keepdims=True)
    total_w = jnp.sum(weight, axis=1, keepdims=True)
    product = jnp.dot(
        jnp.concatenate([weight, weighted], axis=0),
        jnp.concatenate([travel * travel, travel], axis=1),
        precision=highest,
        preferred_element_type=jnp.float32,
    )
    curv = product[:half, :width] - 2.0 * product[half:, width:]
    centered = mean_sum - product[:half, width:]
    logit = -0.5 * (sq_sum + curv - centered * centered / total_w)
    peak = jnp.max(logit, axis=1, keepdims=True)
    total = jnp.sum(jnp.exp(logit - peak), axis=1, keepdims=True)
    logit_ref[...] = logit
    lane = lax.broadcasted_iota(jnp.int32, logit.shape, 1)
    rows = jnp.where(lane == 0, peak, total).T
    stats = jnp.concatenate([rows[:1], rows[1:2]], axis=1)
    for peer in range(stats_ref.shape[0]):
        stats_ref[peer] = stats


def final_kernel(logit_ref, stats_ref, out_ref):
    half = logit_ref.shape[0]
    peaks = stats_ref[:, 0, :half]
    totals = stats_ref[:, 0, half:]
    peak = jnp.max(peaks, axis=0, keepdims=True)
    total = jnp.sum(totals * jnp.exp(peaks - peak), axis=0, keepdims=True)
    row = lax.broadcasted_iota(jnp.int32, (8, peaks.shape[1]), 0)
    columns = jnp.where(row == 0, peak, jnp.log(total)).T
    out_ref[...] = logit_ref[...] - columns[:, :1] - columns[:, 1:2]


vmem = pl.BlockSpec(memory_space=pltpu.VMEM)
hbm = pl.BlockSpec(memory_space=pltpu.HBM)


def in_hbm(x):
    return pltpu.with_memory_space_constraint(x, pltpu.HBM)


def call(kernel, in_specs, out_shape, name, scratch_shapes=(), cost=None):
    return pl.pallas_call(
        kernel,
        in_specs=in_specs,
        out_specs=jax.tree.map(lambda _: vmem, out_shape),
        out_shape=out_shape,
        scratch_shapes=scratch_shapes,
        compiler_params=pltpu.CompilerParams(vmem_limit_bytes=40 << 20),
        name=name,
        cost_estimate=cost,
    )


def per_device(
    cell_index,
    station_xyz,
    w_cell,
    w_station,
    bias_in,
    w_hidden,
    bias_hidden,
    w_out,
    pick_mask,
    arrival,
    quality,
):
    n_cell, n_sta = lax.axis_size("cell"), lax.axis_size("sta")
    events, stations = pick_mask.shape
    cells = cell_index.shape[1]
    f32 = jnp.float32
    shape = jax.ShapeDtypeStruct
    packed = call(
        pack_kernel,
        [hbm] * 3,
        shape((n_cell, 2, stations, events), f32),
        "pack",
        [
            pltpu.VMEM((stations, events), pick_mask.dtype),
            pltpu.VMEM((stations, events), f32),
            pltpu.VMEM((stations, events), f32),
            pltpu.SemaphoreType.DMA((3,)),
        ],
        pl.CostEstimate(flops=2 * 10**9, transcendentals=0, bytes_accessed=10**6),
    )(*[in_hbm(x.T) for x in (pick_mask, arrival, quality)])
    picks = lax.all_to_all(packed, "cell", 0, 0, axis_index_groups=[rotated(n_cell, first_picks)])
    travel = call(
        travel_kernel,
        [vmem] * 6 + [hbm, vmem],
        shape((stations, cells), f32),
        "travel",
        [
            pltpu.VMEM((stations * cells, w_cell.shape[1]), jnp.bfloat16),
            pltpu.VMEM(bias_hidden.shape, f32),
            pltpu.SemaphoreType.DMA,
        ],
    )(
        cell_index,
        station_xyz,
        w_cell,
        w_station,
        bias_in[None],
        w_hidden,
        in_hbm(bias_hidden),
        w_out[None],
    )
    blocks = call(join_kernel, [vmem] * 2, shape((n_cell, 3, stations, cells), f32), "join")(travel, picks)
    equal_cores = [[2 * chip + core for chip in rotated(n_cell, first_blocks)] for core in range(2)]
    pairs = [[2 * chip + core for core in pair_order] for chip in range(n_cell)]
    blocks = lax.all_to_all(blocks, "sta", 0, 0, axis_index_groups=equal_cores)
    blocks = lax.all_gather(blocks, "sta", axis_index_groups=pairs)
    logit, stats = call(
        logit_kernel,
        [vmem],
        (shape((events // 2, cells), f32), shape((n_cell, 1, events), f32)),
        "logit",
    )(blocks)
    stats = lax.all_to_all(stats, "cell", 0, 0, axis_index_groups=[rotated(n_cell, first_stats)])
    return call(final_kernel, [vmem] * 2, shape((events // 2, cells), f32), "final")(logit, stats)


def solution(mesh):
    in_specs = (
        P(None, "cell"),
        P(None, "sta"),
        P(),
        P(),
        P(),
        P(),
        P(),
        P(),
        P("cell", "sta"),
        P("cell", "sta"),
        P("cell", "sta"),
    )
    return jax.shard_map(
        per_device, mesh=mesh, in_specs=in_specs, out_specs=P("sta", "cell"), check_vma=False
    )
```

```python
import jax
import jax.numpy as jnp
from jax import lax
from jax.experimental import pallas as pl
from jax.experimental.pallas import tpu as pltpu
from jax.sharding import PartitionSpec as P

grid_step = 0.015625
first_picks, first_blocks, first_stats = 12, 25, 12
highest = lax.Precision.HIGHEST


def elu(x):
    return jnp.where(x > 0.0, x, jnp.exp(x) - 1.0)


def pack_kernel(
    mask_hbm,
    arrival_hbm,
    quality_hbm,
    cell_hbm,
    station_hbm,
    out_ref,
    cell_ref,
    station_ref,
    mask_ref,
    arrival_ref,
    quality_ref,
    sems,
):
    pairs = (
        (mask_hbm, mask_ref),
        (arrival_hbm, arrival_ref),
        (quality_hbm, quality_ref),
        (cell_hbm, cell_ref),
        (station_hbm, station_ref),
    )
    copies = [pltpu.make_async_copy(*pair, sems.at[k]) for k, pair in enumerate(pairs)]
    for copy in copies:
        copy.start()
    for copy in copies:
        copy.wait()
    weight = mask_ref[...].astype(jnp.float32) * quality_ref[...]
    arrival = arrival_ref[...]
    for peer in range(out_ref.shape[0]):
        out_ref[peer, 0] = weight
        out_ref[peer, 1] = arrival


def travel_kernel(
    cell_ref,
    station_ref,
    w_cell_ref,
    w_station_ref,
    bias_in_ref,
    w_hidden_ref,
    bias_hidden_ref,
    w_out_ref,
    out_ref,
    hidden_ref,
):
    stations = station_ref.shape[1]
    cells = cell_ref.shape[1]
    cell = cell_ref[...].astype(jnp.float32) * grid_step
    cell_columns = cell.T
    station_columns = station_ref[...].T
    cell_rows = jnp.broadcast_to(bias_in_ref[...], (cells, bias_in_ref.shape[1]))
    station_rows = jnp.zeros((stations, bias_in_ref.shape[1]), jnp.float32)
    distance = jnp.zeros((stations, cells), jnp.float32)
    for k in range(3):
        cell_rows = cell_rows + cell_columns[:, k : k + 1] * w_cell_ref[k : k + 1, :]
        station_rows = station_rows + station_columns[:, k : k + 1] * w_station_ref[k : k + 1, :]
        offset = cell[k : k + 1, :] - station_columns[:, k : k + 1]
        distance = distance + offset * offset
    distance = jnp.sqrt(distance)
    for s in range(stations):
        hidden_ref[s * cells : (s + 1) * cells, :] = elu(cell_rows + station_rows[s : s + 1, :]).astype(
            jnp.bfloat16
        )
    hidden = hidden_ref[...]
    for layer in range(w_hidden_ref.shape[0]):
        hidden = elu(
            jnp.dot(hidden, w_hidden_ref[layer], preferred_element_type=jnp.float32)
            + bias_hidden_ref[layer : layer + 1, :]
        ).astype(jnp.bfloat16)
    raw = lax.dot_general(
        w_out_ref[...], hidden, (((1,), (1,)), ((), ())), preferred_element_type=jnp.float32
    )
    raw = jnp.concatenate([raw[:1, s * cells : (s + 1) * cells] for s in range(stations)], axis=0)
    softplus = jnp.maximum(raw, 0.0) + jnp.log1p(jnp.exp(-jnp.abs(raw)))
    out_ref[...] = distance * (0.25 + softplus)


def rotated(count, first):
    return [(first + place) % count for place in range(count)]


def join_kernel(travel_ref, picks_ref, out_ref):
    travel = travel_ref[...]
    peers = out_ref.shape[0]
    for place, member in enumerate(rotated(peers, first_blocks)):
        chip, core = divmod(member, 2)
        out_ref[place, 0] = travel
        w = picks_ref[rotated(peers // 2, first_picks).index(chip), 0]
        a = picks_ref[rotated(peers // 2, first_picks).index(chip), 1]
        half = w.shape[1] // 2
        part = slice(core * half, (core + 1) * half)
        out_ref[place, 1] = jnp.concatenate([w[:, part], a[:, part]], axis=1)


def logit_kernel(blocks_ref, logit_ref, stats_ref):
    peers, _, rows, width = blocks_ref.shape
    half = width // 2
    travel, picks = [
        blocks_ref[:, k].reshape(peers * rows, width) for k in range(2)
    ]
    picks = picks.T
    weight, arrival = picks[:half], picks[half:]
    weighted = weight * arrival
    sq_sum = jnp.sum(weighted * arrival, axis=1, keepdims=True)
    mean_sum = jnp.sum(weighted, axis=1, keepdims=True)
    total_w = jnp.sum(weight, axis=1, keepdims=True)
    product = jnp.dot(
        jnp.concatenate([weight, weighted], axis=0),
        jnp.concatenate([travel * travel, travel], axis=1),
        precision=highest,
        preferred_element_type=jnp.float32,
    )
    curv = product[:half, :width] - 2.0 * product[half:, width:]
    centered = mean_sum - product[:half, width:]
    logit = -0.5 * (sq_sum + curv - centered * centered / total_w)
    peak = jnp.max(logit, axis=1, keepdims=True)
    total = jnp.sum(jnp.exp(logit - peak), axis=1, keepdims=True)
    logit_ref[...] = logit
    lane = lax.broadcasted_iota(jnp.int32, logit.shape, 1)
    rows = jnp.where(lane == 0, peak, total).T
    stats = jnp.concatenate([rows[:1], rows[1:2]], axis=1)
    for peer in range(stats_ref.shape[0]):
        stats_ref[peer] = stats


def final_kernel(logit_ref, stats_ref, out_ref):
    half = logit_ref.shape[0]
    peaks = stats_ref[:, 0, :half]
    totals = stats_ref[:, 0, half:]
    peak = jnp.max(peaks, axis=0, keepdims=True)
    total = jnp.sum(totals * jnp.exp(peaks - peak), axis=0, keepdims=True)
    shift = jnp.broadcast_to(peak + jnp.log(total), (8, half)).T
    out_ref[...] = logit_ref[...] - shift[:, :1]


vmem = pl.BlockSpec(memory_space=pltpu.VMEM)
hbm = pl.BlockSpec(memory_space=pltpu.HBM)


def in_hbm(x):
    return pltpu.with_memory_space_constraint(x, pltpu.HBM)


def call(kernel, in_specs, out_shape, name, scratch_shapes=(), cost=None):
    return pl.pallas_call(
        kernel,
        in_specs=in_specs,
        out_specs=jax.tree.map(lambda _: vmem, out_shape),
        out_shape=out_shape,
        scratch_shapes=scratch_shapes,
        compiler_params=pltpu.CompilerParams(vmem_limit_bytes=40 << 20),
        name=name,
        cost_estimate=cost,
    )


def per_device(
    cell_index,
    station_xyz,
    w_cell,
    w_station,
    bias_in,
    w_hidden,
    bias_hidden,
    w_out,
    pick_mask,
    arrival,
    quality,
):
    n_cell, n_sta = lax.axis_size("cell"), lax.axis_size("sta")
    events, stations = pick_mask.shape
    cells = cell_index.shape[1]
    f32 = jnp.float32
    shape = jax.ShapeDtypeStruct
    packed, cell_index, station_xyz = call(
        pack_kernel,
        [hbm] * 5,
        (
            shape((n_cell, 2, stations, events), f32),
            shape(cell_index.shape, cell_index.dtype),
            shape(station_xyz.shape, f32),
        ),
        "pack",
        [
            pltpu.VMEM((stations, events), pick_mask.dtype),
            pltpu.VMEM((stations, events), f32),
            pltpu.VMEM((stations, events), f32),
            pltpu.SemaphoreType.DMA((5,)),
        ],
        pl.CostEstimate(flops=2 * 10**9, transcendentals=0, bytes_accessed=10**6),
    )(*[in_hbm(x) for x in (pick_mask.T, arrival.T, quality.T, cell_index, station_xyz)])
    picks = lax.all_to_all(packed, "cell", 0, 0, axis_index_groups=[rotated(n_cell, first_picks)])
    travel = call(
        travel_kernel,
        [vmem] * 8,
        shape((stations, cells), f32),
        "travel",
        [pltpu.VMEM((stations * cells, w_cell.shape[1]), jnp.bfloat16)],
    )(
        cell_index,
        station_xyz,
        w_cell,
        w_station,
        bias_in[None],
        w_hidden,
        bias_hidden,
        w_out[None],
    )
    blocks = call(join_kernel, [vmem] * 2, shape((n_sta, 2, stations, cells), f32), "join")(travel, picks)
    blocks = lax.all_to_all(blocks, "sta", 0, 0, axis_index_groups=[rotated(n_sta, first_blocks)])
    logit, stats = call(
        logit_kernel,
        [vmem],
        (shape((events // 2, cells), f32), shape((n_cell, 1, events), f32)),
        "logit",
    )(blocks)
    stats = lax.all_to_all(stats, "cell", 0, 0, axis_index_groups=[rotated(n_cell, first_stats)])
    return call(final_kernel, [vmem] * 2, shape((events // 2, cells), f32), "final")(logit, stats)


def solution(mesh):
    in_specs = (
        P(None, "cell"),
        P(None, "sta"),
        P(),
        P(),
        P(),
        P(),
        P(),
        P(),
        P("cell", "sta"),
        P("cell", "sta"),
        P("cell", "sta"),
    )
    return jax.shard_map(
        per_device, mesh=mesh, in_specs=in_specs, out_specs=P("sta", "cell"), check_vma=False
    )
```

```python
import jax
import jax.numpy as jnp
from jax import lax
from jax.experimental import pallas as pl
from jax.experimental.pallas import tpu as pltpu
from jax.sharding import PartitionSpec as P

grid_step = 0.015625
first_picks, first_blocks, first_stats = 12, 13, 12
pair_order = (0, 1)
highest = lax.Precision.HIGHEST


def elu(x):
    return jnp.where(x > 0.0, x, jnp.exp(x) - 1.0)


def pack_kernel(
    mask_hbm,
    arrival_hbm,
    quality_hbm,
    cell_hbm,
    station_hbm,
    out_ref,
    cell_ref,
    station_ref,
    mask_ref,
    arrival_ref,
    quality_ref,
    sems,
):
    pairs = (
        (mask_hbm, mask_ref),
        (arrival_hbm, arrival_ref),
        (quality_hbm, quality_ref),
        (cell_hbm, cell_ref),
        (station_hbm, station_ref),
    )
    copies = [pltpu.make_async_copy(*pair, sems.at[k]) for k, pair in enumerate(pairs)]
    for copy in copies:
        copy.start()
    for copy in copies:
        copy.wait()
    weight = mask_ref[...].astype(jnp.float32) * quality_ref[...]
    arrival = arrival_ref[...]
    for peer in range(out_ref.shape[0]):
        out_ref[peer, 0] = weight
        out_ref[peer, 1] = arrival


def travel_kernel(
    cell_ref,
    station_ref,
    w_cell_ref,
    w_station_ref,
    bias_in_ref,
    w_hidden_ref,
    bias_hidden_ref,
    w_out_ref,
    out_ref,
    hidden_ref,
):
    stations = station_ref.shape[1]
    cells = cell_ref.shape[1]
    cell = cell_ref[...].astype(jnp.float32) * grid_step
    cell_columns = cell.T
    station_columns = station_ref[...].T
    cell_rows = jnp.broadcast_to(bias_in_ref[...], (cells, bias_in_ref.shape[1]))
    station_rows = jnp.zeros((stations, bias_in_ref.shape[1]), jnp.float32)
    distance = jnp.zeros((stations, cells), jnp.float32)
    for k in range(3):
        cell_rows = cell_rows + cell_columns[:, k : k + 1] * w_cell_ref[k : k + 1, :]
        station_rows = station_rows + station_columns[:, k : k + 1] * w_station_ref[k : k + 1, :]
        offset = cell[k : k + 1, :] - station_columns[:, k : k + 1]
        distance = distance + offset * offset
    distance = jnp.sqrt(distance)
    for s in range(stations):
        hidden_ref[s * cells : (s + 1) * cells, :] = elu(cell_rows + station_rows[s : s + 1, :]).astype(
            jnp.bfloat16
        )
    hidden = hidden_ref[...]
    for layer in range(w_hidden_ref.shape[0]):
        hidden = elu(
            jnp.dot(hidden, w_hidden_ref[layer], preferred_element_type=jnp.float32)
            + bias_hidden_ref[layer : layer + 1, :]
        ).astype(jnp.bfloat16)
    raw = lax.dot_general(
        w_out_ref[...], hidden, (((1,), (1,)), ((), ())), preferred_element_type=jnp.float32
    )
    raw = jnp.concatenate([raw[:1, s * cells : (s + 1) * cells] for s in range(stations)], axis=0)
    softplus = jnp.maximum(raw, 0.0) + jnp.log1p(jnp.exp(-jnp.abs(raw)))
    out_ref[...] = distance * (0.25 + softplus)


def rotated(count, first):
    return [(first + place) % count for place in range(count)]


def join_kernel(travel_ref, picks_ref, out_ref):
    travel = travel_ref[...]
    peers = out_ref.shape[0]
    for place, chip in enumerate(rotated(peers, first_blocks)):
        out_ref[place, 0] = travel
        for k in range(2):
            out_ref[place, 1 + k] = picks_ref[rotated(peers, first_picks).index(chip), k]


def logit_kernel(blocks_ref, logit_ref, stats_ref):
    cores, peers, _, rows, width = blocks_ref.shape
    half = width // 2
    odd = lax.axis_index("sta") % 2 == 1
    travel, weight, arrival = [
        blocks_ref[:, :, k].reshape(cores * peers * rows, width) for k in range(3)
    ]
    weight, arrival = [
        jnp.where(odd, member[half:], member[:half]) for member in (weight.T, arrival.T)
    ]
    weighted = weight * arrival
    sq_sum = jnp.sum(weighted * arrival, axis=1, keepdims=True)
    mean_sum = jnp.sum(weighted, axis=1, keepdims=True)
    total_w = jnp.sum(weight, axis=1, keepdims=True)
    product = jnp.dot(
        jnp.concatenate([weight, weighted], axis=0),
        jnp.concatenate([travel * travel, travel], axis=1),
        precision=highest,
        preferred_element_type=jnp.float32,
    )
    curv = product[:half, :width] - 2.0 * product[half:, width:]
    centered = mean_sum - product[:half, width:]
    logit = -0.5 * (sq_sum + curv - centered * centered / total_w)
    peak = jnp.max(logit, axis=1, keepdims=True)
    total = jnp.sum(jnp.exp(logit - peak), axis=1, keepdims=True)
    logit_ref[...] = logit
    lane = lax.broadcasted_iota(jnp.int32, logit.shape, 1)
    rows = jnp.where(lane == 0, peak, total).T
    stats = jnp.concatenate([rows[:1], rows[1:2]], axis=1)
    for peer in range(stats_ref.shape[0]):
        stats_ref[peer] = stats


def final_kernel(logit_ref, stats_ref, out_ref):
    half = logit_ref.shape[0]
    peaks = stats_ref[:, 0, :half]
    totals = stats_ref[:, 0, half:]
    peak = jnp.max(peaks, axis=0, keepdims=True)
    total = jnp.sum(totals * jnp.exp(peaks - peak), axis=0, keepdims=True)
    shift = jnp.broadcast_to(peak + jnp.log(total), (8, half)).T
    out_ref[...] = logit_ref[...] - shift[:, :1]


vmem = pl.BlockSpec(memory_space=pltpu.VMEM)
hbm = pl.BlockSpec(memory_space=pltpu.HBM)


def in_hbm(x):
    return pltpu.with_memory_space_constraint(x, pltpu.HBM)


def call(kernel, in_specs, out_shape, name, scratch_shapes=(), cost=None):
    return pl.pallas_call(
        kernel,
        in_specs=in_specs,
        out_specs=jax.tree.map(lambda _: vmem, out_shape),
        out_shape=out_shape,
        scratch_shapes=scratch_shapes,
        compiler_params=pltpu.CompilerParams(vmem_limit_bytes=40 << 20),
        name=name,
        cost_estimate=cost,
    )


def per_device(
    cell_index,
    station_xyz,
    w_cell,
    w_station,
    bias_in,
    w_hidden,
    bias_hidden,
    w_out,
    pick_mask,
    arrival,
    quality,
):
    n_cell, n_sta = lax.axis_size("cell"), lax.axis_size("sta")
    events, stations = pick_mask.shape
    cells = cell_index.shape[1]
    f32 = jnp.float32
    shape = jax.ShapeDtypeStruct
    packed, cell_index, station_xyz = call(
        pack_kernel,
        [hbm] * 5,
        (
            shape((n_cell, 2, stations, events), f32),
            shape(cell_index.shape, cell_index.dtype),
            shape(station_xyz.shape, f32),
        ),
        "pack",
        [
            pltpu.VMEM((stations, events), pick_mask.dtype),
            pltpu.VMEM((stations, events), f32),
            pltpu.VMEM((stations, events), f32),
            pltpu.SemaphoreType.DMA((5,)),
        ],
        pl.CostEstimate(flops=2 * 10**9, transcendentals=0, bytes_accessed=10**6),
    )(*[in_hbm(x) for x in (pick_mask.T, arrival.T, quality.T, cell_index, station_xyz)])
    picks = lax.all_to_all(packed, "cell", 0, 0, axis_index_groups=[rotated(n_cell, first_picks)])
    travel = call(
        travel_kernel,
        [vmem] * 8,
        shape((stations, cells), f32),
        "travel",
        [pltpu.VMEM((stations * cells, w_cell.shape[1]), jnp.bfloat16)],
    )(
        cell_index,
        station_xyz,
        w_cell,
        w_station,
        bias_in[None],
        w_hidden,
        bias_hidden,
        w_out[None],
    )
    blocks = call(join_kernel, [vmem] * 2, shape((n_cell, 3, stations, cells), f32), "join")(travel, picks)
    equal_cores = [[2 * chip + core for chip in rotated(n_cell, first_blocks)] for core in range(2)]
    pairs = [[2 * chip + core for core in pair_order] for chip in range(n_cell)]
    blocks = lax.all_to_all(blocks, "sta", 0, 0, axis_index_groups=equal_cores)
    blocks = lax.all_gather(blocks, "sta", axis_index_groups=pairs)
    logit, stats = call(
        logit_kernel,
        [vmem],
        (shape((events // 2, cells), f32), shape((n_cell, 1, events), f32)),
        "logit",
    )(blocks)
    stats = lax.all_to_all(stats, "cell", 0, 0, axis_index_groups=[rotated(n_cell, first_stats)])
    return call(final_kernel, [vmem] * 2, shape((events // 2, cells), f32), "final")(logit, stats)


def solution(mesh):
    in_specs = (
        P(None, "cell"),
        P(None, "sta"),
        P(),
        P(),
        P(),
        P(),
        P(),
        P(),
        P("cell", "sta"),
        P("cell", "sta"),
        P("cell", "sta"),
    )
    return jax.shard_map(
        per_device, mesh=mesh, in_specs=in_specs, out_specs=P("sta", "cell"), check_vma=False
    )
```

```python
import jax
import jax.numpy as jnp
from jax import lax
from jax.experimental import pallas as pl
from jax.experimental.pallas import tpu as pltpu
from jax.sharding import PartitionSpec as P

grid_step = 0.015625
first_picks, first_blocks, first_stats = 13, 13, 12
pair_order = (0, 1)
highest = lax.Precision.HIGHEST


def elu(x):
    return jnp.where(x > 0.0, x, jnp.exp(x) - 1.0)


def pack_kernel(
    mask_hbm,
    arrival_hbm,
    quality_hbm,
    cell_hbm,
    station_hbm,
    out_ref,
    cell_ref,
    station_ref,
    mask_ref,
    arrival_ref,
    quality_ref,
    sems,
):
    pairs = (
        (mask_hbm, mask_ref),
        (arrival_hbm, arrival_ref),
        (quality_hbm, quality_ref),
        (cell_hbm, cell_ref),
        (station_hbm, station_ref),
    )
    copies = [pltpu.make_async_copy(*pair, sems.at[k]) for k, pair in enumerate(pairs)]
    for copy in copies:
        copy.start()
    for copy in copies:
        copy.wait()
    weight = mask_ref[...].astype(jnp.float32) * quality_ref[...]
    arrival = arrival_ref[...]
    for peer in range(out_ref.shape[0]):
        out_ref[peer, 0] = weight
        out_ref[peer, 1] = arrival


def travel_kernel(
    cell_ref,
    station_ref,
    w_cell_ref,
    w_station_ref,
    bias_in_ref,
    w_hidden_ref,
    bias_hidden_ref,
    w_out_ref,
    out_ref,
    hidden_ref,
):
    stations = station_ref.shape[1]
    cells = cell_ref.shape[1]
    cell = cell_ref[...].astype(jnp.float32) * grid_step
    cell_columns = cell.T
    station_columns = station_ref[...].T
    cell_rows = jnp.broadcast_to(bias_in_ref[...], (cells, bias_in_ref.shape[1]))
    station_rows = jnp.zeros((stations, bias_in_ref.shape[1]), jnp.float32)
    distance = jnp.zeros((stations, cells), jnp.float32)
    for k in range(3):
        cell_rows = cell_rows + cell_columns[:, k : k + 1] * w_cell_ref[k : k + 1, :]
        station_rows = station_rows + station_columns[:, k : k + 1] * w_station_ref[k : k + 1, :]
        offset = cell[k : k + 1, :] - station_columns[:, k : k + 1]
        distance = distance + offset * offset
    distance = jnp.sqrt(distance)
    for s in range(stations):
        hidden_ref[s * cells : (s + 1) * cells, :] = elu(cell_rows + station_rows[s : s + 1, :]).astype(
            jnp.bfloat16
        )
    hidden = hidden_ref[...]
    for layer in range(w_hidden_ref.shape[0]):
        hidden = elu(
            jnp.dot(hidden, w_hidden_ref[layer], preferred_element_type=jnp.float32)
            + bias_hidden_ref[layer : layer + 1, :]
        ).astype(jnp.bfloat16)
    raw = lax.dot_general(
        w_out_ref[...], hidden, (((1,), (1,)), ((), ())), preferred_element_type=jnp.float32
    )
    raw = jnp.concatenate([raw[:1, s * cells : (s + 1) * cells] for s in range(stations)], axis=0)
    softplus = jnp.maximum(raw, 0.0) + jnp.log1p(jnp.exp(-jnp.abs(raw)))
    out_ref[...] = distance * (0.25 + softplus)


def rotated(count, first):
    return [(first + place) % count for place in range(count)]


def join_kernel(travel_ref, picks_ref, out_ref):
    travel = travel_ref[...]
    peers = out_ref.shape[0]
    for place, chip in enumerate(rotated(peers, first_blocks)):
        out_ref[place, 0] = travel
        for k in range(2):
            out_ref[place, 1 + k] = picks_ref[rotated(peers, first_picks).index(chip), k]


def logit_kernel(blocks_ref, logit_ref, stats_ref):
    cores, peers, _, rows, width = blocks_ref.shape
    half = width // 2
    odd = lax.axis_index("sta") % 2 == 1
    travel, weight, arrival = [
        blocks_ref[:, :, k].reshape(cores * peers * rows, width) for k in range(3)
    ]
    weight, arrival = [
        jnp.where(odd, member[half:], member[:half]) for member in (weight.T, arrival.T)
    ]
    weighted = weight * arrival
    sq_sum = jnp.sum(weighted * arrival, axis=1, keepdims=True)
    mean_sum = jnp.sum(weighted, axis=1, keepdims=True)
    total_w = jnp.sum(weight, axis=1, keepdims=True)
    product = jnp.dot(
        jnp.concatenate([weight, weighted], axis=0),
        jnp.concatenate([travel * travel, travel], axis=1),
        precision=highest,
        preferred_element_type=jnp.float32,
    )
    curv = product[:half, :width] - 2.0 * product[half:, width:]
    centered = mean_sum - product[:half, width:]
    logit = -0.5 * (sq_sum + curv - centered * centered / total_w)
    peak = jnp.max(logit, axis=1, keepdims=True)
    total = jnp.sum(jnp.exp(logit - peak), axis=1, keepdims=True)
    logit_ref[...] = logit
    lane = lax.broadcasted_iota(jnp.int32, logit.shape, 1)
    rows = jnp.where(lane == 0, peak, total).T
    stats = jnp.concatenate([rows[:1], rows[1:2]], axis=1)
    for peer in range(stats_ref.shape[0]):
        stats_ref[peer] = stats


def final_kernel(logit_ref, stats_ref, out_ref):
    half = logit_ref.shape[0]
    peaks = stats_ref[:, 0, :half]
    totals = stats_ref[:, 0, half:]
    peak = jnp.max(peaks, axis=0, keepdims=True)
    total = jnp.sum(totals * jnp.exp(peaks - peak), axis=0, keepdims=True)
    shift = jnp.broadcast_to(peak + jnp.log(total), (8, half)).T
    out_ref[...] = logit_ref[...] - shift[:, :1]


vmem = pl.BlockSpec(memory_space=pltpu.VMEM)
hbm = pl.BlockSpec(memory_space=pltpu.HBM)


def in_hbm(x):
    return pltpu.with_memory_space_constraint(x, pltpu.HBM)


def call(kernel, in_specs, out_shape, name, scratch_shapes=(), cost=None):
    return pl.pallas_call(
        kernel,
        in_specs=in_specs,
        out_specs=jax.tree.map(lambda _: vmem, out_shape),
        out_shape=out_shape,
        scratch_shapes=scratch_shapes,
        compiler_params=pltpu.CompilerParams(vmem_limit_bytes=40 << 20),
        name=name,
        cost_estimate=cost,
    )


def per_device(
    cell_index,
    station_xyz,
    w_cell,
    w_station,
    bias_in,
    w_hidden,
    bias_hidden,
    w_out,
    pick_mask,
    arrival,
    quality,
):
    n_cell, n_sta = lax.axis_size("cell"), lax.axis_size("sta")
    events, stations = pick_mask.shape
    cells = cell_index.shape[1]
    f32 = jnp.float32
    shape = jax.ShapeDtypeStruct
    packed, cell_index, station_xyz = call(
        pack_kernel,
        [hbm] * 5,
        (
            shape((n_cell, 2, stations, events), f32),
            shape(cell_index.shape, cell_index.dtype),
            shape(station_xyz.shape, f32),
        ),
        "pack",
        [
            pltpu.VMEM((stations, events), pick_mask.dtype),
            pltpu.VMEM((stations, events), f32),
            pltpu.VMEM((stations, events), f32),
            pltpu.SemaphoreType.DMA((5,)),
        ],
        pl.CostEstimate(flops=2 * 10**9, transcendentals=0, bytes_accessed=10**6),
    )(*[in_hbm(x) for x in (pick_mask.T, arrival.T, quality.T, cell_index, station_xyz)])
    picks = lax.all_to_all(packed, "cell", 0, 0, axis_index_groups=[rotated(n_cell, first_picks)])
    travel = call(
        travel_kernel,
        [vmem] * 8,
        shape((stations, cells), f32),
        "travel",
        [pltpu.VMEM((stations * cells, w_cell.shape[1]), jnp.bfloat16)],
    )(
        cell_index,
        station_xyz,
        w_cell,
        w_station,
        bias_in[None],
        w_hidden,
        bias_hidden,
        w_out[None],
    )
    blocks = call(join_kernel, [vmem] * 2, shape((n_cell, 3, stations, cells), f32), "join")(travel, picks)
    equal_cores = [[2 * chip + core for chip in rotated(n_cell, first_blocks)] for core in range(2)]
    pairs = [[2 * chip + core for core in pair_order] for chip in range(n_cell)]
    blocks = lax.all_to_all(blocks, "sta", 0, 0, axis_index_groups=equal_cores)
    blocks = lax.all_gather(blocks, "sta", axis_index_groups=pairs)
    logit, stats = call(
        logit_kernel,
        [vmem],
        (shape((events // 2, cells), f32), shape((n_cell, 1, events), f32)),
        "logit",
    )(blocks)
    stats = lax.all_to_all(stats, "cell", 0, 0, axis_index_groups=[rotated(n_cell, first_stats)])
    return call(final_kernel, [vmem] * 2, shape((events // 2, cells), f32), "final")(logit, stats)


def solution(mesh):
    in_specs = (
        P(None, "cell"),
        P(None, "sta"),
        P(),
        P(),
        P(),
        P(),
        P(),
        P(),
        P("cell", "sta"),
        P("cell", "sta"),
        P("cell", "sta"),
    )
    return jax.shard_map(
        per_device, mesh=mesh, in_specs=in_specs, out_specs=P("sta", "cell"), check_vma=False
    )
```

```python
import jax
import jax.numpy as jnp
from jax import lax
from jax.experimental import pallas as pl
from jax.experimental.pallas import tpu as pltpu
from jax.sharding import PartitionSpec as P

grid_step = 0.015625
first_picks, first_blocks, first_stats = 13, 13, 12
pair_order = (0, 1)
highest = lax.Precision.HIGHEST


def elu(x):
    return jnp.where(x > 0.0, x, jnp.exp(x) - 1.0)


def pack_kernel(
    mask_hbm,
    arrival_hbm,
    quality_hbm,
    cell_hbm,
    station_hbm,
    w_cell_hbm,
    out_ref,
    cell_ref,
    station_ref,
    w_cell_ref,
    mask_ref,
    arrival_ref,
    quality_ref,
    sems,
):
    pairs = (
        (mask_hbm, mask_ref),
        (arrival_hbm, arrival_ref),
        (quality_hbm, quality_ref),
        (cell_hbm, cell_ref),
        (station_hbm, station_ref),
        (w_cell_hbm, w_cell_ref),
    )
    copies = [pltpu.make_async_copy(*pair, sems.at[k]) for k, pair in enumerate(pairs)]
    for copy in copies:
        copy.start()
    for copy in copies:
        copy.wait()
    weight = mask_ref[...].astype(jnp.float32) * quality_ref[...]
    arrival = arrival_ref[...]
    for peer in range(out_ref.shape[0]):
        out_ref[peer, 0] = weight
        out_ref[peer, 1] = arrival


def travel_kernel(
    cell_ref,
    station_ref,
    w_cell_ref,
    w_station_ref,
    bias_in_ref,
    w_hidden_ref,
    bias_hidden_ref,
    w_out_ref,
    out_ref,
    hidden_ref,
):
    stations = station_ref.shape[1]
    cells = cell_ref.shape[1]
    cell = cell_ref[...].astype(jnp.float32) * grid_step
    cell_columns = cell.T
    station_columns = station_ref[...].T
    cell_rows = jnp.broadcast_to(bias_in_ref[...], (cells, bias_in_ref.shape[1]))
    station_rows = jnp.zeros((stations, bias_in_ref.shape[1]), jnp.float32)
    distance = jnp.zeros((stations, cells), jnp.float32)
    for k in range(3):
        cell_rows = cell_rows + cell_columns[:, k : k + 1] * w_cell_ref[k : k + 1, :]
        station_rows = station_rows + station_columns[:, k : k + 1] * w_station_ref[k : k + 1, :]
        offset = cell[k : k + 1, :] - station_columns[:, k : k + 1]
        distance = distance + offset * offset
    distance = jnp.sqrt(distance)
    for s in range(stations):
        hidden_ref[s * cells : (s + 1) * cells, :] = elu(cell_rows + station_rows[s : s + 1, :]).astype(
            jnp.bfloat16
        )
    hidden = hidden_ref[...]
    for layer in range(w_hidden_ref.shape[0]):
        hidden = elu(
            jnp.dot(hidden, w_hidden_ref[layer], preferred_element_type=jnp.float32)
            + bias_hidden_ref[layer : layer + 1, :]
        ).astype(jnp.bfloat16)
    raw = lax.dot_general(
        w_out_ref[...], hidden, (((1,), (1,)), ((), ())), preferred_element_type=jnp.float32
    )
    raw = jnp.concatenate([raw[:1, s * cells : (s + 1) * cells] for s in range(stations)], axis=0)
    softplus = jnp.maximum(raw, 0.0) + jnp.log1p(jnp.exp(-jnp.abs(raw)))
    out_ref[...] = distance * (0.25 + softplus)


def rotated(count, first):
    return [(first + place) % count for place in range(count)]


def join_kernel(travel_ref, picks_ref, out_ref):
    travel = travel_ref[...]
    peers = out_ref.shape[0]
    for place, chip in enumerate(rotated(peers, first_blocks)):
        out_ref[place, 0] = travel
        for k in range(2):
            out_ref[place, 1 + k] = picks_ref[rotated(peers, first_picks).index(chip), k]


def logit_kernel(blocks_ref, logit_ref, stats_ref):
    cores, peers, _, rows, width = blocks_ref.shape
    half = width // 2
    odd = lax.axis_index("sta") % 2 == 1
    travel, weight, arrival = [
        blocks_ref[:, :, k].reshape(cores * peers * rows, width) for k in range(3)
    ]
    weight, arrival = [
        jnp.where(odd, member[half:], member[:half]) for member in (weight.T, arrival.T)
    ]
    weighted = weight * arrival
    sq_sum = jnp.sum(weighted * arrival, axis=1, keepdims=True)
    mean_sum = jnp.sum(weighted, axis=1, keepdims=True)
    total_w = jnp.sum(weight, axis=1, keepdims=True)
    product = jnp.dot(
        jnp.concatenate([weight, weighted], axis=0),
        jnp.concatenate([travel * travel, travel], axis=1),
        precision=highest,
        preferred_element_type=jnp.float32,
    )
    curv = product[:half, :width] - 2.0 * product[half:, width:]
    centered = mean_sum - product[:half, width:]
    logit = -0.5 * (sq_sum + curv - centered * centered / total_w)
    peak = jnp.max(logit, axis=1, keepdims=True)
    total = jnp.sum(jnp.exp(logit - peak), axis=1, keepdims=True)
    logit_ref[...] = logit
    lane = lax.broadcasted_iota(jnp.int32, logit.shape, 1)
    rows = jnp.where(lane == 0, peak, total).T
    stats = jnp.concatenate([rows[:1], rows[1:2]], axis=1)
    for peer in range(stats_ref.shape[0]):
        stats_ref[peer] = stats


def final_kernel(logit_ref, stats_ref, out_ref):
    half = logit_ref.shape[0]
    peaks = stats_ref[:, 0, :half]
    totals = stats_ref[:, 0, half:]
    peak = jnp.max(peaks, axis=0, keepdims=True)
    total = jnp.sum(totals * jnp.exp(peaks - peak), axis=0, keepdims=True)
    shift = jnp.broadcast_to(peak + jnp.log(total), (8, half)).T
    out_ref[...] = logit_ref[...] - shift[:, :1]


vmem = pl.BlockSpec(memory_space=pltpu.VMEM)
hbm = pl.BlockSpec(memory_space=pltpu.HBM)


def in_hbm(x):
    return pltpu.with_memory_space_constraint(x, pltpu.HBM)


def call(kernel, in_specs, out_shape, name, scratch_shapes=(), cost=None):
    return pl.pallas_call(
        kernel,
        in_specs=in_specs,
        out_specs=jax.tree.map(lambda _: vmem, out_shape),
        out_shape=out_shape,
        scratch_shapes=scratch_shapes,
        compiler_params=pltpu.CompilerParams(vmem_limit_bytes=40 << 20),
        name=name,
        cost_estimate=cost,
    )


def per_device(
    cell_index,
    station_xyz,
    w_cell,
    w_station,
    bias_in,
    w_hidden,
    bias_hidden,
    w_out,
    pick_mask,
    arrival,
    quality,
):
    n_cell, n_sta = lax.axis_size("cell"), lax.axis_size("sta")
    events, stations = pick_mask.shape
    cells = cell_index.shape[1]
    f32 = jnp.float32
    shape = jax.ShapeDtypeStruct
    packed, cell_index, station_xyz, w_cell = call(
        pack_kernel,
        [hbm] * 6,
        (
            shape((n_cell, 2, stations, events), f32),
            shape(cell_index.shape, cell_index.dtype),
            shape(station_xyz.shape, f32),
            shape(w_cell.shape, f32),
        ),
        "pack",
        [
            pltpu.VMEM((stations, events), pick_mask.dtype),
            pltpu.VMEM((stations, events), f32),
            pltpu.VMEM((stations, events), f32),
            pltpu.SemaphoreType.DMA((6,)),
        ],
        pl.CostEstimate(flops=2 * 10**9, transcendentals=0, bytes_accessed=10**6),
    )(*[in_hbm(x) for x in (pick_mask.T, arrival.T, quality.T, cell_index, station_xyz, w_cell)])
    picks = lax.all_to_all(packed, "cell", 0, 0, axis_index_groups=[rotated(n_cell, first_picks)])
    travel = call(
        travel_kernel,
        [vmem] * 8,
        shape((stations, cells), f32),
        "travel",
        [pltpu.VMEM((stations * cells, w_cell.shape[1]), jnp.bfloat16)],
    )(
        cell_index,
        station_xyz,
        w_cell,
        w_station,
        bias_in[None],
        w_hidden,
        bias_hidden,
        w_out[None],
    )
    blocks = call(join_kernel, [vmem] * 2, shape((n_cell, 3, stations, cells), f32), "join")(travel, picks)
    equal_cores = [[2 * chip + core for chip in rotated(n_cell, first_blocks)] for core in range(2)]
    pairs = [[2 * chip + core for core in pair_order] for chip in range(n_cell)]
    blocks = lax.all_to_all(blocks, "sta", 0, 0, axis_index_groups=equal_cores)
    blocks = lax.all_gather(blocks, "sta", axis_index_groups=pairs)
    logit, stats = call(
        logit_kernel,
        [vmem],
        (shape((events // 2, cells), f32), shape((n_cell, 1, events), f32)),
        "logit",
    )(blocks)
    stats = lax.all_to_all(stats, "cell", 0, 0, axis_index_groups=[rotated(n_cell, first_stats)])
    return call(final_kernel, [vmem] * 2, shape((events // 2, cells), f32), "final")(logit, stats)


def solution(mesh):
    in_specs = (
        P(None, "cell"),
        P(None, "sta"),
        P(),
        P(),
        P(),
        P(),
        P(),
        P(),
        P("cell", "sta"),
        P("cell", "sta"),
        P("cell", "sta"),
    )
    return jax.shard_map(
        per_device, mesh=mesh, in_specs=in_specs, out_specs=P("sta", "cell"), check_vma=False
    )
```
